32 devices in a mesh: lon: 4 (over y, x), lat: 8 (over z, core).
Axes of the slice: x: 2, y: 2, z: 4, core: 2. Of those that a mesh axis runs over, the one named last changes fastest.
Arguments:
- field: float32 [32, 768, 3072], P(None, 'lat', 'lon'), may hold values from -6 to 6
- vertical: float32 [32, 32], replicated, may hold values from -1.5 to 1.5, as said below
- rate: float32 [32, 768], P(None, 'lat'), may hold values from 3.2552085e-05 to 0.5
- lat_kernel: float32 [768, 768], replicated, may hold values from 0 to 1, as said below
Outputs:
- increment: float32 [32, 768, 3072], P(None, 'lat', 'lon')
The draws below stay inside these ranges and needn't reach their ends.
Inputs may be any that keep to these rules, and one draw needn't show every extreme that they name: `vertical`: the identity plus independent terms of magnitude at most 0.5 times 4 / sqrt(32). `lat_kernel`: Non-negative weights.
All inputs are finite; a program needn't handle non-finite values.
Results may differ from the reference program's by a relative error of at most 0.00015.
Values sent between devices are 32-bit elements; how exact they have to be, the bound alone decides.
A program may use at most 128 MiB of HBM per device.

```python
import math
import jax
import jax.numpy as jnp
from jax import lax

LEV = 32
NLAT = 768
NLON = 3072
PASSES = 2


def draw_vertical(key, part):
    noise = jnp.clip(jax.random.normal(key, (LEV, LEV), jnp.float32), -4.0, 4.0)
    return jnp.eye(LEV, dtype=jnp.float32) + 0.5 * noise / jnp.sqrt(jnp.float32(LEV))


def draw_lat_kernel(key, part):
    width = NLAT / 8.0
    rows = jnp.arange(NLAT, dtype=jnp.float32)[:, None]
    cols = jnp.arange(NLAT, dtype=jnp.float32)[None, :]
    base = jnp.exp(-0.5 * ((rows - cols) / width) ** 2) / (width * 2.5066)
    factors = jnp.exp(jax.random.uniform(key, (NLAT, NLAT), jnp.float32, -0.6931, 0.6931))
    return base * factors + 0.5 * jnp.eye(NLAT, dtype=jnp.float32)


def steps_of(key, dims, shards, least, high):
    factor_of, own = 1.0, jax.random.fold_in(key, 6)
    for dim, shards_of in shards:
        heights = jnp.exp(jax.random.uniform(jax.random.fold_in(own, dim), (shards_of,), jnp.float32, least / len(shards), high / len(shards)))
        factor_of = factor_of * jnp.repeat(heights, dims[dim] // shards_of).reshape([-1 if axis == dim else 1 for axis in range(len(dims))])
    return factor_of


def normal_values(rng, extent, scale, reach, cuts=(), held_as=jnp.bfloat16):
    factor_of = steps_of(rng, extent, cuts, -0.22, 0.18) if cuts else 1.0
    result = jax.random.normal(rng, extent, jnp.float32) * scale * factor_of
    return jnp.minimum(jnp.maximum(result, -reach), reach).astype(held_as)


def setup_inputs(seed: int = 0) -> dict:
    arg_keys = jax.random.split(jax.random.key(seed), 5)
    field = normal_values(arg_keys[0], (LEV, NLAT, NLON), 1.0, 6.0, ((1, 8), (2, 4)), jnp.float32)
    vertical = draw_vertical(jax.random.fold_in(arg_keys[4], 71), 0)
    rate = jnp.clip(jnp.exp(math.log(0.5) - 9.639522 * jax.random.uniform(arg_keys[2], (LEV, NLAT), jnp.float32) ** steps_of(arg_keys[2], (LEV, NLAT), ((1, 8),), -0.2, 0.2)), 3.255208503105678e-05, 0.5)
    lat_kernel = draw_lat_kernel(jax.random.fold_in(arg_keys[4], 71), 0)
    return {"field": field, "vertical": vertical, "rate": rate, "lat_kernel": lat_kernel}


def combine(first, second):
    return (first[0] * second[0], second[0] * first[1] + second[1])


def one_level(items):
    rows, level_rate, kernel = items
    log_decay = jnp.log1p(-level_rate)[:, None]
    decay = jnp.exp(log_decay)
    coefficient = level_rate[:, None]
    positions = jnp.arange(NLON, dtype=jnp.float32)[None, :]
    closing = -jnp.expm1(NLON * log_decay[:, 0])
    decays = jnp.broadcast_to(decay, rows.shape)
    for step in range(PASSES):
        east = step % 2 == 0
        filtered = lax.associative_scan(combine, (decays, coefficient * rows), axis=1, reverse=not east)[1]
        if east:
            edge = filtered[:, -1]
            power = jnp.exp((positions + 1.0) * log_decay)
        else:
            edge = filtered[:, 0]
            power = jnp.exp((NLON - positions) * log_decay)
        rows = filtered + power * (edge / closing)[:, None]
    return jnp.dot(kernel, rows, precision=lax.Precision.HIGHEST)


def reference(field, vertical, rate, lat_kernel):
    mixed = jnp.einsum("km,mjn->kjn", vertical, field, precision=lax.Precision.HIGHEST)
    return lax.map(lambda pair: one_level((pair[0], pair[1], lat_kernel)), (mixed, rate))
```

```python
import functools

import jax
import jax.numpy as jnp
from jax import lax
from jax.experimental import pallas as pl
from jax.experimental.pallas import tpu as pltpu
from jax.sharding import PartitionSpec as P

MESH = pl.DeviceIdType.MESH
LANES = 128
SUB = 8


def partner(me, step, count):
    index, bit = 0, 1
    while bit < count:
        digit = lax.rem(me // bit, 2)
        if step & bit:
            digit = 1 - digit
        index = index + digit * bit
        bit *= 2
    return index


def steps_far_first(count):
    order, top = [], count
    while top > 1:
        order += list(range(top // 2, top))
        top //= 2
    return order


def split(value):
    high = value.astype(jnp.bfloat16)
    low = (value - high.astype(jnp.float32)).astype(jnp.bfloat16)
    return high, low


def dot3(a_high, a_low, b):
    high, low = split(b)
    dot = functools.partial(jnp.dot, preferred_element_type=jnp.float32)
    return dot(a_high, high) + (dot(a_high, low) + dot(a_low, high))


def kernel(
    n_lon, n_lat,
    field, mixer, packed, weights, out,
    mix_high, mix_low, w_high, w_low, rows, edges, edges_in, state, gathered, smooth,
    edge_send, edge_recv, x_send, x_recv, y_send, y_recv, own_sem,
):
    lon, lat = lax.axis_index("lon"), lax.axis_index("lat")
    rounds, levels, depth, width = rows.shape
    groups, chunks = depth // SUB, width // LANES
    order = steps_far_first(n_lat)
    lane = lax.broadcasted_iota(jnp.int32, (SUB, LANES), 1)
    ahead = (lane + 1).astype(jnp.float32)
    behind = (LANES - lane).astype(jnp.float32)

    barrier = pltpu.get_barrier_semaphore()
    for step in range(1, n_lon):
        pl.semaphore_signal(barrier, inc=1, device_id={"lon": lax.rem(lon + step, n_lon)}, device_id_type=MESH)
    for step in order:
        pl.semaphore_signal(barrier, inc=1, device_id={"lat": partner(lat, step, n_lat)}, device_id_type=MESH)

    def pick(values, index):
        one = jnp.sum(jnp.where(lane == index, values, 0.0), axis=1, keepdims=True)
        return jnp.broadcast_to(one, (SUB, LANES))

    def column(values, index):
        return jnp.broadcast_to(values[:, index : index + 1], (SUB, LANES))

    def group_rows(g):
        return pl.ds(pl.multiple_of(g * SUB, SUB), SUB)

    def edge_copy(q, step):
        return pltpu.make_async_remote_copy(
            src_ref=edges.at[q], dst_ref=edges_in.at[q, step - 1],
            send_sem=edge_send.at[q, step - 1], recv_sem=edge_recv.at[q, step - 1],
            device_id={"lon": lax.rem(lon + step, n_lon)}, device_id_type=MESH,
        )

    def x_copy(q, step):
        target = partner(lat, step, n_lat)
        return pltpu.make_async_remote_copy(
            src_ref=rows.at[q, target],
            dst_ref=gathered.at[q, pl.ds(pl.multiple_of(lat * depth, SUB), depth)],
            send_sem=x_send.at[q, step - 1], recv_sem=x_recv.at[q, step - 1],
            device_id={"lat": target}, device_id_type=MESH,
        )

    def y_copy(q, step):
        target = partner(lat, step, n_lat)
        return pltpu.make_async_remote_copy(
            src_ref=smooth.at[q, pl.ds(pl.multiple_of(target * depth, SUB), depth)],
            dst_ref=out.at[lat * rounds + q],
            send_sem=y_send.at[q, step - 1], recv_sem=y_recv.at[q, step - 1],
            device_id={"lat": target}, device_id_type=MESH,
        )

    def own_copy(q):
        return pltpu.make_async_copy(
            smooth.at[q, pl.ds(pl.multiple_of(lat * depth, SUB), depth)],
            out.at[lat * rounds + q], own_sem.at[q],
        )

    for q in range(rounds):
        mix_high[q], mix_low[q] = split(mixer[q])

    def scan_group(q, g):
        here = group_rows(g)
        x = field[:, here, :]
        x = x.reshape(x.shape[0] * SUB, width)
        mixed = dot3(mix_high[q], mix_low[q], x)
        rows[q, :, here, :] = mixed.reshape(levels, SUB, width)
        logs = packed[0, q, here, :]

        def level(t, acc):
            log = pick(logs, 2 * t)
            power = jnp.exp(log)
            east, west = [], []
            for k in range(7):
                east.append(jnp.where(lane >= 2**k, power, 0.0))
                west.append(jnp.where(lane < LANES - 2**k, power, 0.0))
                power = power * power
            stride = jnp.exp(log * float(LANES))
            to_east, to_west = jnp.exp(log * ahead), jnp.exp(log * behind)
            sums, ys, zs = [], [], []
            for c in range(chunks):
                v = rows[q, t, here, c * LANES : (c + 1) * LANES]
                y = z = v
                for k in range(7):
                    y = y + east[k] * pltpu.roll(y, 2**k, 1)
                    z = z + west[k] * pltpu.roll(z, LANES - 2**k, 1)
                ys.append(column(y, LANES - 1))
                zs.append(column(z, 0))
                sums.append(y + z - v)
            carry = ys[0]
            for c in range(1, chunks):
                sums[c] = sums[c] + to_east * carry
                carry = ys[c] + stride * carry
            back = zs[chunks - 1]
            for c in range(chunks - 2, -1, -1):
                sums[c] = sums[c] + to_west * back
                back = zs[c] + stride * back
            for c in range(chunks):
                rows[q, t, here, c * LANES : (c + 1) * LANES] = sums[c]
            return jnp.where(lane == 2 * t, carry, jnp.where(lane == 2 * t + 1, back, acc))

        edges[q, here, :] = lax.fori_loop(0, levels, level, jnp.zeros((SUB, LANES), jnp.float32))

    def state_group(q, g):
        here = group_rows(g)
        log = packed[0, q, here, :] * float(width)
        eastward = lax.rem(lane, 2) == 0
        total = edges[q, here, :] * jnp.exp(log * float(n_lon - 1))
        for step in range(1, n_lon):
            hops = jnp.where(eastward, float(step - 1), float(n_lon - step - 1))
            total = total + edges_in[q, step - 1, here, :] * jnp.exp(log * hops)
        state[here, :] = total / (1.0 - jnp.exp(log * float(n_lon)))

    def correct(q, step):
        t = partner(lat, step, n_lat)

        def group(g, _):
            here = group_rows(g)
            log = pick(packed[0, q, here, :], 2 * t)
            scale = pick(packed[1, q, here, :], 2 * t)
            incoming = state[here, :]
            carry = pick(incoming, 2 * t) * scale
            back = pick(incoming, 2 * t + 1) * scale
            stride = jnp.exp(log * float(LANES))
            to_east, to_west = jnp.exp(log * ahead), jnp.exp(log * behind)
            parts = []
            for c in range(chunks):
                parts.append(scale * rows[q, t, here, c * LANES : (c + 1) * LANES] + to_east * carry)
                carry = carry * stride
            for c in range(chunks - 1, -1, -1):
                parts[c] = parts[c] + to_west * back
                back = back * stride
            for c in range(chunks):
                at = slice(c * LANES, (c + 1) * LANES)
                if step == 0:
                    gathered[q, pl.ds(pl.multiple_of(lat * depth + g * SUB, SUB), SUB), at] = parts[c]
                else:
                    rows[q, t, here, at] = parts[c]
            return 0

        lax.fori_loop(0, groups, group, 0)

    def first(q, _):
        def scan(g, _):
            scan_group(q, g)
            return 0

        lax.fori_loop(0, groups, scan, 0)

        @pl.when(q == 0)
        def _():
            pl.semaphore_wait(barrier, n_lon - 1 + n_lat - 1)

        for step in range(1, n_lon):
            edge_copy(q, step).start()
        for step in range(1, n_lon):
            edge_copy(q, step).wait()

        def states(g, _):
            state_group(q, g)
            return 0

        lax.fori_loop(0, groups, states, 0)
        for step in order:
            correct(q, step)
            x_copy(q, step).start()
        correct(q, 0)
        return 0

    lax.fori_loop(0, rounds, first, 0)
    w_high[...], w_low[...] = split(weights[...])

    def second(q, _):
        for step in order:
            x_copy(q, step).wait_recv()
        tile = 256 if width % 256 == 0 else LANES

        def columns(n, _):
            at = pl.ds(pl.multiple_of(n * tile, tile), tile)
            smooth[q, :, at] = dot3(w_high[...], w_low[...], gathered[q, :, at])
            return 0

        lax.fori_loop(0, width // tile, columns, 0)
        for step in order:
            y_copy(q, step).start()
        own_copy(q).start()
        return 0

    lax.fori_loop(0, rounds, second, 0)

    def finish(q, _):
        own_copy(q).wait()
        for step in order:
            x_copy(q, step).wait_send()
            y_copy(q, step).wait()
        return 0

    lax.fori_loop(0, rounds, finish, 0)


def on_device(n_lon, n_lat, field, vertical, rate, lat_kernel):
    lev, depth, width = field.shape
    total = depth * n_lat
    rounds = lev // n_lat
    f32, bf16 = jnp.float32, jnp.bfloat16
    by_round = vertical.reshape(n_lat, rounds, lev).transpose(1, 0, 2)
    mixer = (by_round[:, :, None, :, None] * jnp.eye(SUB, dtype=f32)[None, None, :, None, :]).reshape(
        rounds, n_lat * SUB, lev * SUB
    )
    pair = jnp.stack([jnp.log1p(-rate), rate / (2.0 - rate)])
    pair = pair.reshape(2, n_lat, rounds, depth).transpose(0, 2, 3, 1)
    packed = jnp.pad(jnp.repeat(pair, 2, axis=3), ((0, 0), (0, 0), (0, 0), (0, LANES - 2 * n_lat)), constant_values=-1.0)
    vmem, dma = pltpu.VMEM, pltpu.SemaphoreType.DMA
    return pl.pallas_call(
        functools.partial(kernel, n_lon, n_lat),
        out_shape=jax.ShapeDtypeStruct(field.shape, f32),
        in_specs=[pl.BlockSpec(memory_space=pltpu.VMEM)] * 4,
        out_specs=pl.BlockSpec(memory_space=pl.ANY),
        scratch_shapes=[
            vmem((rounds, n_lat * SUB, lev * SUB), bf16),
            vmem((rounds, n_lat * SUB, lev * SUB), bf16),
            vmem((total, total), bf16),
            vmem((total, total), bf16),
            vmem((rounds, n_lat, depth, width), f32),
            vmem((rounds, depth, LANES), f32),
            vmem((rounds, n_lon - 1, depth, LANES), f32),
            vmem((depth, LANES), f32),
            vmem((rounds, total, width), f32),
            vmem((rounds, total, width), f32),
            dma((rounds, n_lon - 1)),
            dma((rounds, n_lon - 1)),
            dma((rounds, n_lat - 1)),
            dma((rounds, n_lat - 1)),
            dma((rounds, n_lat - 1)),
            dma((rounds, n_lat - 1)),
            dma((rounds,)),
        ],
        compiler_params=pltpu.CompilerParams(
            collective_id=0, has_side_effects=True, vmem_limit_bytes=60 * 1024 * 1024
        ),
        cost_estimate=pl.CostEstimate(
            flops=6 * lev * depth * width * (total + lev), bytes_accessed=8 * lev * depth * width, transcendentals=0
        ),
    )(field, mixer, packed, lat_kernel)


def solution(mesh):
    return jax.shard_map(
        functools.partial(on_device, mesh.shape["lon"], mesh.shape["lat"]),
        mesh=mesh,
        in_specs=(P(None, "lat", "lon"), P(), P(None, "lat"), P()),
        out_specs=P(None, "lat", "lon"),
        check_vma=False,
    )
```

```python
import functools

import jax
import jax.numpy as jnp
from jax import lax
from jax.experimental import pallas as pl
from jax.experimental.pallas import tpu as pltpu
from jax.sharding import PartitionSpec as P

MESH = pl.DeviceIdType.MESH
LANES = 128
SUB = 8


def partner(me, step, count):
    index, bit = 0, 1
    while bit < count:
        index = index + lax.rem(me // bit + step // bit, 2) * bit
        bit *= 2
    return index


def step_at(me, place, count):
    turn = lax.rem(me, count // 2)
    return lax.rem(place - turn + count - 1, count - 1) + 1


def split(value):
    high = value.astype(jnp.bfloat16)
    low = (value - high.astype(jnp.float32)).astype(jnp.bfloat16)
    return high, low


def dot3(a_high, a_low, b):
    high, low = split(b)
    dot = functools.partial(jnp.dot, preferred_element_type=jnp.float32)
    return dot(a_high, high) + (dot(a_high, low) + dot(a_low, high))


def kernel(
    n_lon, n_lat,
    field_hbm, vertical, packed, weights_hbm, out,
    field, weights, mix_high, mix_low, w_high, w_low, rows, edges, edges_in, state, gathered, smooth,
    edge_send, edge_recv, x_send, x_recv, y_send, y_recv, own_sem, field_sem, weights_sem,
):
    lon, lat = lax.axis_index("lon"), lax.axis_index("lat")
    rounds, levels, depth, width = rows.shape
    groups, chunks = depth // SUB, width // LANES
    order = range(1, n_lat)
    lane = lax.broadcasted_iota(jnp.int32, (SUB, LANES), 1)
    ahead = (lane + 1).astype(jnp.float32)
    behind = (LANES - lane).astype(jnp.float32)

    barrier = pltpu.get_barrier_semaphore()
    for step in range(1, n_lon):
        pl.semaphore_signal(barrier, inc=1, device_id={"lon": lax.rem(lon + step, n_lon)}, device_id_type=MESH)
    for step in order:
        pl.semaphore_signal(barrier, inc=1, device_id={"lat": partner(lat, step, n_lat)}, device_id_type=MESH)

    def pick(values, index):
        one = jnp.sum(jnp.where(lane == index, values, 0.0), axis=1, keepdims=True)
        return jnp.broadcast_to(one, (SUB, LANES))

    def column(values, index):
        return jnp.broadcast_to(values[:, index : index + 1], (SUB, LANES))

    def group_rows(g):
        return pl.ds(pl.multiple_of(g * SUB, SUB), SUB)

    def edge_copy(q, step):
        return pltpu.make_async_remote_copy(
            src_ref=edges.at[q], dst_ref=edges_in.at[q, step - 1],
            send_sem=edge_send.at[q, step - 1], recv_sem=edge_recv.at[q, step - 1],
            device_id={"lon": lax.rem(lon + step, n_lon)}, device_id_type=MESH,
        )

    def x_copy(q, step):
        target = partner(lat, step, n_lat)
        return pltpu.make_async_remote_copy(
            src_ref=rows.at[q, target],
            dst_ref=gathered.at[q, pl.ds(pl.multiple_of(lat * depth, SUB), depth)],
            send_sem=x_send.at[q, step - 1], recv_sem=x_recv.at[q, step - 1],
            device_id={"lat": target}, device_id_type=MESH,
        )

    def y_copy(q, step):
        target = partner(lat, step, n_lat)
        return pltpu.make_async_remote_copy(
            src_ref=smooth.at[q, pl.ds(pl.multiple_of(target * depth, SUB), depth)],
            dst_ref=out.at[lat * rounds + q],
            send_sem=y_send.at[q, step - 1], recv_sem=y_recv.at[q, step - 1],
            device_id={"lat": target}, device_id_type=MESH,
        )

    def own_copy(q):
        return pltpu.make_async_copy(
            smooth.at[q, pl.ds(pl.multiple_of(lat * depth, SUB), depth)],
            out.at[lat * rounds + q], own_sem.at[q],
        )

    def field_copy(g):
        return pltpu.make_async_copy(
            field_hbm.at[:, group_rows(g), :], field.at[:, group_rows(g), :], field_sem.at[g]
        )

    def load(g, _):
        field_copy(g).start()
        return 0

    weights_copy = pltpu.make_async_copy(weights_hbm, weights, weights_sem)
    lax.fori_loop(0, groups, load, 0)
    weights_copy.start()

    wide, lev = levels * SUB, vertical.shape[0]
    one_hot = lambda hit: jnp.where(hit, 1.0, 0.0).astype(jnp.bfloat16)
    dot = functools.partial(jnp.dot, preferred_element_type=jnp.float32)
    iota = lambda shape, axis: lax.broadcasted_iota(jnp.int32, shape, axis)
    spread = one_hot(iota((lev, lev * SUB), 0) == lax.shift_right_logical(iota((lev, lev * SUB), 1), 3))
    grid = (wide, lev * SUB)
    same = lax.bitwise_and(iota(grid, 0), SUB - 1) == lax.bitwise_and(iota(grid, 1), SUB - 1)
    for q in range(rounds):
        chosen = one_hot(lax.shift_right_logical(iota((wide, lev), 0), 3) * rounds + q == iota((wide, lev), 1))
        for half, target in zip(split(vertical[...]), (mix_high, mix_low)):
            picked = dot(chosen, half).astype(jnp.bfloat16)
            target[q] = jnp.where(same, dot(picked, spread), 0.0).astype(jnp.bfloat16)

    def scan_group(q, g):
        here = group_rows(g)
        x = field[:, here, :]
        x = x.reshape(x.shape[0] * SUB, width)
        mixed = dot3(mix_high[q], mix_low[q], x)
        rows[q, :, here, :] = mixed.reshape(levels, SUB, width)
        logs = packed[0, q, here, :]

        def level(t, acc):
            log = pick(logs, 2 * t)
            power = jnp.exp(log)
            east, west = [], []
            for k in range(7):
                east.append(jnp.where(lane >= 2**k, power, 0.0))
                west.append(jnp.where(lane < LANES - 2**k, power, 0.0))
                power = power * power
            stride = jnp.exp(log * float(LANES))
            to_east, to_west = jnp.exp(log * ahead), jnp.exp(log * behind)
            sums, ys, zs = [], [], []
            for c in range(chunks):
                v = rows[q, t, here, c * LANES : (c + 1) * LANES]
                y = z = v
                for k in range(7):
                    y = y + east[k] * pltpu.roll(y, 2**k, 1)
                    z = z + west[k] * pltpu.roll(z, LANES - 2**k, 1)
                ys.append(column(y, LANES - 1))
                zs.append(column(z, 0))
                sums.append(y + z - v)
            carry = ys[0]
            for c in range(1, chunks):
                sums[c] = sums[c] + to_east * carry
                carry = ys[c] + stride * carry
            back = zs[chunks - 1]
            for c in range(chunks - 2, -1, -1):
                sums[c] = sums[c] + to_west * back
                back = zs[c] + stride * back
            for c in range(chunks):
                rows[q, t, here, c * LANES : (c + 1) * LANES] = sums[c]
            return jnp.where(lane == 2 * t, carry, jnp.where(lane == 2 * t + 1, back, acc))

        edges[q, here, :] = lax.fori_loop(0, levels, level, jnp.zeros((SUB, LANES), jnp.float32))

    def state_group(q, g):
        here = group_rows(g)
        log = packed[0, q, here, :] * float(width)
        eastward = lax.rem(lane, 2) == 0
        total = edges[q, here, :] * jnp.exp(log * float(n_lon - 1))
        for step in range(1, n_lon):
            hops = jnp.where(eastward, float(step - 1), float(n_lon - step - 1))
            total = total + edges_in[q, step - 1, here, :] * jnp.exp(log * hops)
        state[here, :] = total / (1.0 - jnp.exp(log * float(n_lon)))

    def set_row(q, t, g, at, part):
        rows[q, t, group_rows(g), at] = part

    def set_own(q, g, at, part):
        gathered[q, pl.ds(pl.multiple_of(lat * depth + g * SUB, SUB), SUB), at] = part

    def correct(q, t, store):
        def group(g, _):
            here = group_rows(g)
            log = pick(packed[0, q, here, :], 2 * t)
            scale = pick(packed[1, q, here, :], 2 * t)
            incoming = state[here, :]
            carry = pick(incoming, 2 * t) * scale
            back = pick(incoming, 2 * t + 1) * scale
            stride = jnp.exp(log * float(LANES))
            to_east, to_west = jnp.exp(log * ahead), jnp.exp(log * behind)
            parts = []
            for c in range(chunks):
                parts.append(scale * rows[q, t, here, c * LANES : (c + 1) * LANES] + to_east * carry)
                carry = carry * stride
            for c in range(chunks - 1, -1, -1):
                parts[c] = parts[c] + to_west * back
                back = back * stride
            for c in range(chunks):
                at = slice(c * LANES, (c + 1) * LANES)
                store(g, at, parts[c])
            return 0

        lax.fori_loop(0, groups, group, 0)

    def first(q, _):
        def scan(g, _):
            @pl.when(q == 0)
            def _():
                field_copy(g).wait()

            scan_group(q, g)
            return 0

        lax.fori_loop(0, groups, scan, 0)

        @pl.when(q == 0)
        def _():
            pl.semaphore_wait(barrier, n_lon - 1 + n_lat - 1)

        for step in range(1, n_lon):
            edge_copy(q, step).start()
        for step in range(1, n_lon):
            edge_copy(q, step).wait()

        def states(g, _):
            state_group(q, g)
            return 0

        lax.fori_loop(0, groups, states, 0)

        def ship(place, _):
            step = step_at(lat, place, n_lat)
            t = partner(lat, step, n_lat)
            correct(q, t, lambda g, at, part: set_row(q, t, g, at, part))
            x_copy(q, step).start()
            return 0

        lax.fori_loop(0, n_lat - 1, ship, 0)
        correct(q, lat, lambda g, at, part: set_own(q, g, at, part))
        return 0

    lax.fori_loop(0, rounds, first, 0)
    weights_copy.wait()
    w_high[...], w_low[...] = split(weights[...])

    def second(q, _):
        for step in order:
            x_copy(q, step).wait_recv()
        tile = 256 if width % 256 == 0 else LANES

        def columns(n, _):
            at = pl.ds(pl.multiple_of(n * tile, tile), tile)
            smooth[q, :, at] = dot3(w_high[...], w_low[...], gathered[q, :, at])
            return 0

        lax.fori_loop(0, width // tile, columns, 0)

        def ship(place, _):
            y_copy(q, step_at(lat, place, n_lat)).start()
            return 0

        lax.fori_loop(0, n_lat - 1, ship, 0)
        own_copy(q).start()
        return 0

    lax.fori_loop(0, rounds, second, 0)

    def finish(q, _):
        own_copy(q).wait()
        for step in order:
            x_copy(q, step).wait_send()
            y_copy(q, step).wait()
        return 0

    lax.fori_loop(0, rounds, finish, 0)


def on_device(n_lon, n_lat, field, vertical, rate, lat_kernel):
    lev, depth, width = field.shape
    total = depth * n_lat
    rounds = lev // n_lat
    f32, bf16 = jnp.float32, jnp.bfloat16
    pair = jnp.stack([jnp.log1p(-rate), rate / (2.0 - rate)])
    pair = pair.reshape(2, n_lat, rounds, depth).transpose(0, 2, 3, 1)
    packed = jnp.pad(jnp.repeat(pair, 2, axis=3), ((0, 0), (0, 0), (0, 0), (0, LANES - 2 * n_lat)), constant_values=-1.0)
    vmem, dma = pltpu.VMEM, pltpu.SemaphoreType.DMA
    return pl.pallas_call(
        functools.partial(kernel, n_lon, n_lat),
        out_shape=jax.ShapeDtypeStruct(field.shape, f32),
        in_specs=[
            pl.BlockSpec(memory_space=pl.ANY),
            pl.BlockSpec(memory_space=pltpu.VMEM),
            pl.BlockSpec(memory_space=pltpu.VMEM),
            pl.BlockSpec(memory_space=pl.ANY),
        ],
        out_specs=pl.BlockSpec(memory_space=pl.ANY),
        scratch_shapes=[
            vmem(field.shape, f32),
            vmem((total, total), f32),
            vmem((rounds, n_lat * SUB, lev * SUB), bf16),
            vmem((rounds, n_lat * SUB, lev * SUB), bf16),
            vmem((total, total), bf16),
            vmem((total, total), bf16),
            vmem((rounds, n_lat, depth, width), f32),
            vmem((rounds, depth, LANES), f32),
            vmem((rounds, n_lon - 1, depth, LANES), f32),
            vmem((depth, LANES), f32),
            vmem((rounds, total, width), f32),
            vmem((rounds, total, width), f32),
            dma((rounds, n_lon - 1)),
            dma((rounds, n_lon - 1)),
            dma((rounds, n_lat - 1)),
            dma((rounds, n_lat - 1)),
            dma((rounds, n_lat - 1)),
            dma((rounds, n_lat - 1)),
            dma((rounds,)),
            dma((depth // SUB,)),
            dma(()),
        ],
        compiler_params=pltpu.CompilerParams(
            collective_id=0, has_side_effects=True, vmem_limit_bytes=60 * 1024 * 1024
        ),
        cost_estimate=pl.CostEstimate(
            flops=6 * lev * depth * width * (total + lev), bytes_accessed=8 * lev * depth * width, transcendentals=0
        ),
    )(field, vertical, packed, lat_kernel)


def solution(mesh):
    return jax.shard_map(
        functools.partial(on_device, mesh.shape["lon"], mesh.shape["lat"]),
        mesh=mesh,
        in_specs=(P(None, "lat", "lon"), P(), P(None, "lat"), P()),
        out_specs=P(None, "lat", "lon"),
        check_vma=False,
    )
```

```python
import functools

import jax
import jax.numpy as jnp
from jax import lax
from jax.experimental import pallas as pl
from jax.experimental.pallas import tpu as pltpu
from jax.sharding import PartitionSpec as P

MESH = pl.DeviceIdType.MESH
LANES = 128
SUB = 8


def partner(me, step, count):
    index, bit = 0, 1
    while bit < count:
        index = index + lax.rem(me // bit + step // bit, 2) * bit
        bit *= 2
    return index


def step_at(me, place, count):
    turn = lax.rem(me, count // 2)
    return lax.rem(place - turn + count - 1, count - 1) + 1


def split(value):
    high = value.astype(jnp.bfloat16)
    low = (value - high.astype(jnp.float32)).astype(jnp.bfloat16)
    return high, low


def dot3(a_high, a_low, b):
    high, low = split(b)
    dot = functools.partial(jnp.dot, preferred_element_type=jnp.float32)
    return dot(a_high, high) + (dot(a_high, low) + dot(a_low, high))


def kernel(
    n_lon, n_lat,
    field_hbm, vertical, packed, weights_hbm, out,
    field, weights, mix_high, mix_low, w_high, w_low, rows, edges, edges_in, state, gathered, smooth,
    edge_send, edge_recv, x_send, x_recv, y_send, y_recv, own_sem, field_sem, weights_sem,
):
    lon, lat = lax.axis_index("lon"), lax.axis_index("lat")
    rounds, levels, depth, width = rows.shape
    groups, chunks = depth // SUB, width // LANES
    order = range(1, n_lat)

    barrier = pltpu.get_barrier_semaphore()
    for step in range(1, n_lon):
        pl.semaphore_signal(barrier, inc=1, device_id={"lon": lax.rem(lon + step, n_lon)}, device_id_type=MESH)
    for step in order:
        pl.semaphore_signal(barrier, inc=1, device_id={"lat": partner(lat, step, n_lat)}, device_id_type=MESH)

    def group_rows(g):
        return pl.ds(pl.multiple_of(g * SUB, SUB), SUB)

    def edge_copy(q, step):
        return pltpu.make_async_remote_copy(
            src_ref=edges.at[q], dst_ref=edges_in.at[q, step - 1],
            send_sem=edge_send.at[q, step - 1], recv_sem=edge_recv.at[q, step - 1],
            device_id={"lon": lax.rem(lon + step, n_lon)}, device_id_type=MESH,
        )

    def x_copy(q, step):
        target = partner(lat, step, n_lat)
        return pltpu.make_async_remote_copy(
            src_ref=rows.at[q, target],
            dst_ref=gathered.at[q, pl.ds(pl.multiple_of(lat * depth, SUB), depth)],
            send_sem=x_send.at[q, step - 1], recv_sem=x_recv.at[q, step - 1],
            device_id={"lat": target}, device_id_type=MESH,
        )

    def y_copy(q, step):
        target = partner(lat, step, n_lat)
        return pltpu.make_async_remote_copy(
            src_ref=smooth.at[q, pl.ds(pl.multiple_of(target * depth, SUB), depth)],
            dst_ref=out.at[lat * rounds + q],
            send_sem=y_send.at[q, step - 1], recv_sem=y_recv.at[q, step - 1],
            device_id={"lat": target}, device_id_type=MESH,
        )

    def own_copy(q):
        return pltpu.make_async_copy(
            smooth.at[q, pl.ds(pl.multiple_of(lat * depth, SUB), depth)],
            out.at[lat * rounds + q], own_sem.at[q],
        )

    def field_copy(g):
        return pltpu.make_async_copy(
            field_hbm.at[:, group_rows(g), :], field.at[:, group_rows(g), :], field_sem.at[g]
        )

    def load(g, _):
        field_copy(g).start()
        return 0

    weights_copy = pltpu.make_async_copy(weights_hbm, weights, weights_sem)
    lax.fori_loop(0, groups, load, 0)
    weights_copy.start()

    wide, lev = levels * SUB, vertical.shape[0]
    one_hot = lambda hit: jnp.where(hit, 1.0, 0.0).astype(jnp.bfloat16)
    dot = functools.partial(jnp.dot, preferred_element_type=jnp.float32)
    iota = lambda shape, axis: lax.broadcasted_iota(jnp.int32, shape, axis)
    spread = one_hot(iota((lev, lev * SUB), 0) == lax.shift_right_logical(iota((lev, lev * SUB), 1), 3))
    grid = (wide, lev * SUB)
    same = lax.bitwise_and(iota(grid, 0), SUB - 1) == lax.bitwise_and(iota(grid, 1), SUB - 1)
    for q in range(rounds):
        chosen = one_hot(lax.shift_right_logical(iota((wide, lev), 0), 3) * rounds + q == iota((wide, lev), 1))
        for half, target in zip(split(vertical[...]), (mix_high, mix_low)):
            picked = dot(chosen, half).astype(jnp.bfloat16)
            target[q] = jnp.where(same, dot(picked, spread), 0.0).astype(jnp.bfloat16)

    def spread_lane(values, index):
        one = jnp.sum(jnp.where(lane_of(values) == index, values, 0.0), axis=1, keepdims=True)
        return jnp.broadcast_to(one, values.shape)

    def lane_of(values):
        return lax.broadcasted_iota(jnp.int32, values.shape, 1)

    def column(values, index):
        return jnp.broadcast_to(values[:, index : index + 1], values.shape)

    def powers(log):
        place = lane_of(log)
        ahead = (place + 1).astype(jnp.float32)
        behind = (LANES - place).astype(jnp.float32)
        return jnp.exp(log * float(LANES)), jnp.exp(log * ahead), jnp.exp(log * behind)

    def scan_group(q, g):
        here = group_rows(g)
        x = field[:, here, :]
        x = x.reshape(x.shape[0] * SUB, width)
        mixed = dot3(mix_high[q], mix_low[q], x)
        logs = packed[0, q, here, :]
        log = jnp.concatenate([spread_lane(logs, 2 * t) for t in range(levels)], axis=0)
        stride, to_east, to_west = powers(log)
        place = lane_of(log)
        power = jnp.exp(log)
        east, west = [], []
        for k in range(7):
            east.append(jnp.where(place >= 2**k, power, 0.0))
            west.append(jnp.where(place < LANES - 2**k, power, 0.0))
            power = power * power
        sums, ys, zs = [], [], []
        for c in range(chunks):
            v = mixed[:, c * LANES : (c + 1) * LANES]
            y = z = v
            for k in range(7):
                y = y + east[k] * pltpu.roll(y, 2**k, 1)
                z = z + west[k] * pltpu.roll(z, LANES - 2**k, 1)
            ys.append(column(y, LANES - 1))
            zs.append(column(z, 0))
            sums.append(y + z - v)
        carry = ys[0]
        for c in range(1, chunks):
            sums[c] = sums[c] + to_east * carry
            carry = ys[c] + stride * carry
        back = zs[chunks - 1]
        for c in range(chunks - 2, -1, -1):
            sums[c] = sums[c] + to_west * back
            back = zs[c] + stride * back
        for c in range(chunks):
            rows[q, :, here, c * LANES : (c + 1) * LANES] = sums[c].reshape(levels, SUB, LANES)
        edge = jnp.zeros((SUB, LANES), jnp.float32)
        lane = lane_of(edge)
        for t in range(levels):
            part = slice(t * SUB, (t + 1) * SUB)
            edge = jnp.where(lane == 2 * t, carry[part], jnp.where(lane == 2 * t + 1, back[part], edge))
        edges[q, here, :] = edge

    def find_state(q):
        log = packed[0, q] * float(width)
        eastward = lax.rem(lane_of(log), 2) == 0
        total = edges[q] * jnp.exp(log * float(n_lon - 1))
        for step in range(1, n_lon):
            hops = jnp.where(eastward, float(step - 1), float(n_lon - step - 1))
            total = total + edges_in[q, step - 1] * jnp.exp(log * hops)
        state[...] = total / (1.0 - jnp.exp(log * float(n_lon)))

    def set_row(q, t, at, part):
        rows[q, t, :, at] = part

    def set_own(q, at, part):
        gathered[q, pl.ds(pl.multiple_of(lat * depth, SUB), depth), at] = part

    def correct(q, t, store):
        incoming = state[...]
        scale = spread_lane(packed[1, q], 2 * t)
        stride, to_east, to_west = powers(spread_lane(packed[0, q], 2 * t))
        carry = spread_lane(incoming, 2 * t) * scale
        back = spread_lane(incoming, 2 * t + 1) * scale
        parts = []
        for c in range(chunks):
            parts.append(scale * rows[q, t, :, c * LANES : (c + 1) * LANES] + to_east * carry)
            carry = carry * stride
        for c in range(chunks - 1, -1, -1):
            parts[c] = parts[c] + to_west * back
            back = back * stride
        for c in range(chunks):
            store(slice(c * LANES, (c + 1) * LANES), parts[c])

    def first(q, _):
        def scan(g, _):
            @pl.when(q == 0)
            def _():
                field_copy(g).wait()

            scan_group(q, g)
            return 0

        lax.fori_loop(0, groups, scan, 0)

        @pl.when(q == 0)
        def _():
            pl.semaphore_wait(barrier, n_lon - 1 + n_lat - 1)

        for step in range(1, n_lon):
            edge_copy(q, step).start()
        for step in range(1, n_lon):
            edge_copy(q, step).wait()

        find_state(q)

        def ship(place, _):
            step = step_at(lat, place, n_lat)
            t = partner(lat, step, n_lat)
            correct(q, t, functools.partial(set_row, q, t))
            x_copy(q, step).start()
            return 0

        lax.fori_loop(0, n_lat - 1, ship, 0)
        correct(q, lat, functools.partial(set_own, q))
        return 0

    lax.fori_loop(0, rounds, first, 0)
    weights_copy.wait()
    w_high[...], w_low[...] = split(weights[...])

    def second(q, _):
        for step in order:
            x_copy(q, step).wait_recv()
        tile = 256 if width % 256 == 0 else LANES

        def columns(n, _):
            at = pl.ds(pl.multiple_of(n * tile, tile), tile)
            smooth[q, :, at] = dot3(w_high[...], w_low[...], gathered[q, :, at])
            return 0

        lax.fori_loop(0, width // tile, columns, 0)

        def ship(place, _):
            y_copy(q, step_at(lat, place, n_lat)).start()
            return 0

        lax.fori_loop(0, n_lat - 1, ship, 0)
        own_copy(q).start()
        return 0

    lax.fori_loop(0, rounds, second, 0)

    def finish(q, _):
        own_copy(q).wait()
        for step in order:
            x_copy(q, step).wait_send()
            y_copy(q, step).wait()
        return 0

    lax.fori_loop(0, rounds, finish, 0)


def on_device(n_lon, n_lat, field, vertical, rate, lat_kernel):
    lev, depth, width = field.shape
    total = depth * n_lat
    rounds = lev // n_lat
    f32, bf16 = jnp.float32, jnp.bfloat16
    pair = jnp.stack([jnp.log1p(-rate), rate / (2.0 - rate)])
    pair = pair.reshape(2, n_lat, rounds, depth).transpose(0, 2, 3, 1)
    packed = jnp.pad(jnp.repeat(pair, 2, axis=3), ((0, 0), (0, 0), (0, 0), (0, LANES - 2 * n_lat)), constant_values=-1.0)
    vmem, dma = pltpu.VMEM, pltpu.SemaphoreType.DMA
    return pl.pallas_call(
        functools.partial(kernel, n_lon, n_lat),
        out_shape=jax.ShapeDtypeStruct(field.shape, f32),
        in_specs=[
            pl.BlockSpec(memory_space=pl.ANY),
            pl.BlockSpec(memory_space=pltpu.VMEM),
            pl.BlockSpec(memory_space=pltpu.VMEM),
            pl.BlockSpec(memory_space=pl.ANY),
        ],
        out_specs=pl.BlockSpec(memory_space=pl.ANY),
        scratch_shapes=[
            vmem(field.shape, f32),
            vmem((total, total), f32),
            vmem((rounds, n_lat * SUB, lev * SUB), bf16),
            vmem((rounds, n_lat * SUB, lev * SUB), bf16),
            vmem((total, total), bf16),
            vmem((total, total), bf16),
            vmem((rounds, n_lat, depth, width), f32),
            vmem((rounds, depth, LANES), f32),
            vmem((rounds, n_lon - 1, depth, LANES), f32),
            vmem((depth, LANES), f32),
            vmem((rounds, total, width), f32),
            vmem((rounds, total, width), f32),
            dma((rounds, n_lon - 1)),
            dma((rounds, n_lon - 1)),
            dma((rounds, n_lat - 1)),
            dma((rounds, n_lat - 1)),
            dma((rounds, n_lat - 1)),
            dma((rounds, n_lat - 1)),
            dma((rounds,)),
            dma((depth // SUB,)),
            dma(()),
        ],
        compiler_params=pltpu.CompilerParams(
            collective_id=0, has_side_effects=True, vmem_limit_bytes=60 * 1024 * 1024
        ),
        cost_estimate=pl.CostEstimate(
            flops=6 * lev * depth * width * (total + lev), bytes_accessed=8 * lev * depth * width, transcendentals=0
        ),
    )(field, vertical, packed, lat_kernel)


def solution(mesh):
    return jax.shard_map(
        functools.partial(on_device, mesh.shape["lon"], mesh.shape["lat"]),
        mesh=mesh,
        in_specs=(P(None, "lat", "lon"), P(), P(None, "lat"), P()),
        out_specs=P(None, "lat", "lon"),
        check_vma=False,
    )
```

```python
import functools

import jax
import jax.numpy as jnp
from jax import lax
from jax.experimental import pallas as pl
from jax.experimental.pallas import tpu as pltpu
from jax.sharding import PartitionSpec as P

MESH = pl.DeviceIdType.MESH
LANES = 128
SUB = 8


def partner(me, step, count):
    index, bit = 0, 1
    while bit < count:
        index = index + lax.rem(me // bit + step // bit, 2) * bit
        bit *= 2
    return index


def step_at(me, place, count):
    turn = lax.rem(me, count // 2)
    return lax.rem(place - turn + count - 1, count - 1) + 1


def split(value):
    high = value.astype(jnp.bfloat16)
    low = (value - high.astype(jnp.float32)).astype(jnp.bfloat16)
    return high, low


def dot3(a_high, a_low, b):
    high, low = split(b)
    dot = functools.partial(jnp.dot, preferred_element_type=jnp.float32)
    return dot(a_high, high) + (dot(a_high, low) + dot(a_low, high))


def kernel(
    n_lon, n_lat,
    field_hbm, vertical, packed, weights_hbm, out,
    field, weights, mix_high, mix_low, w_high, w_low, rows, edges, edges_in, state, gathered, smooth,
    edge_send, edge_recv, x_send, x_recv, y_send, y_recv, own_sem, field_sem, weights_sem,
):
    lon, lat = lax.axis_index("lon"), lax.axis_index("lat")
    rounds, levels, depth, width = rows.shape
    groups, chunks = depth // SUB, width // LANES
    parts = x_send.shape[1]
    part = depth // parts
    order = range(1, n_lat)

    barrier = pltpu.get_barrier_semaphore()
    for step in range(1, n_lon):
        pl.semaphore_signal(barrier, inc=1, device_id={"lon": lax.rem(lon + step, n_lon)}, device_id_type=MESH)
    for step in order:
        pl.semaphore_signal(barrier, inc=1, device_id={"lat": partner(lat, step, n_lat)}, device_id_type=MESH)

    def group_rows(g):
        return pl.ds(pl.multiple_of(g * SUB, SUB), SUB)

    def part_rows(h):
        return pl.ds(pl.multiple_of(h * part, SUB), part)

    def part_gathered(h):
        return pl.ds(pl.multiple_of(lat * depth + h * part, SUB), part)

    def edge_copy(q, h, step):
        return pltpu.make_async_remote_copy(
            src_ref=edges.at[q, part_rows(h)], dst_ref=edges_in.at[q, step - 1, part_rows(h)],
            send_sem=edge_send.at[q, h, step - 1], recv_sem=edge_recv.at[q, h, step - 1],
            device_id={"lon": lax.rem(lon + step, n_lon)}, device_id_type=MESH,
        )

    def x_copy(q, h, step):
        target = partner(lat, step, n_lat)
        return pltpu.make_async_remote_copy(
            src_ref=rows.at[q, target, part_rows(h)], dst_ref=gathered.at[q, part_gathered(h)],
            send_sem=x_send.at[q, h, step - 1], recv_sem=x_recv.at[q, h, step - 1],
            device_id={"lat": target}, device_id_type=MESH,
        )

    def y_copy(q, step):
        target = partner(lat, step, n_lat)
        return pltpu.make_async_remote_copy(
            src_ref=smooth.at[q, pl.ds(pl.multiple_of(target * depth, SUB), depth)],
            dst_ref=out.at[lat * rounds + q],
            send_sem=y_send.at[q, step - 1], recv_sem=y_recv.at[q, step - 1],
            device_id={"lat": target}, device_id_type=MESH,
        )

    def own_copy(q):
        return pltpu.make_async_copy(
            smooth.at[q, pl.ds(pl.multiple_of(lat * depth, SUB), depth)],
            out.at[lat * rounds + q], own_sem.at[q],
        )

    def field_copy(g):
        return pltpu.make_async_copy(
            field_hbm.at[:, group_rows(g), :], field.at[:, group_rows(g), :], field_sem.at[g]
        )

    def load(g, _):
        field_copy(g).start()
        return 0

    weights_copy = pltpu.make_async_copy(weights_hbm, weights, weights_sem)
    lax.fori_loop(0, groups, load, 0)
    weights_copy.start()

    wide, lev = levels * SUB, vertical.shape[0]
    one_hot = lambda hit: jnp.where(hit, 1.0, 0.0).astype(jnp.bfloat16)
    dot = functools.partial(jnp.dot, preferred_element_type=jnp.float32)
    iota = lambda shape, axis: lax.broadcasted_iota(jnp.int32, shape, axis)
    spread = one_hot(iota((lev, lev * SUB), 0) == lax.shift_right_logical(iota((lev, lev * SUB), 1), 3))
    grid = (wide, lev * SUB)
    same = lax.bitwise_and(iota(grid, 0), SUB - 1) == lax.bitwise_and(iota(grid, 1), SUB - 1)
    for q in range(rounds):
        chosen = one_hot(lax.shift_right_logical(iota((wide, lev), 0), 3) * rounds + q == iota((wide, lev), 1))
        for half, target in zip(split(vertical[...]), (mix_high, mix_low)):
            picked = dot(chosen, half).astype(jnp.bfloat16)
            target[q] = jnp.where(same, dot(picked, spread), 0.0).astype(jnp.bfloat16)

    def spread_lane(values, index):
        one = jnp.sum(jnp.where(lane_of(values) == index, values, 0.0), axis=1, keepdims=True)
        return jnp.broadcast_to(one, values.shape)

    def lane_of(values):
        return lax.broadcasted_iota(jnp.int32, values.shape, 1)

    def column(values, index):
        return jnp.broadcast_to(values[:, index : index + 1], values.shape)

    def powers(log):
        place = lane_of(log)
        ahead = (place + 1).astype(jnp.float32)
        behind = (LANES - place).astype(jnp.float32)
        return jnp.exp(log * float(LANES)), jnp.exp(log * ahead), jnp.exp(log * behind)

    def scan_group(q, g):
        here = group_rows(g)
        x = field[:, here, :]
        x = x.reshape(x.shape[0] * SUB, width)
        mixed = dot3(mix_high[q], mix_low[q], x)
        logs = packed[0, q, here, :]
        log = jnp.concatenate([spread_lane(logs, 2 * t) for t in range(levels)], axis=0)
        stride, to_east, to_west = powers(log)
        place = lane_of(log)
        power = jnp.exp(log)
        east, west = [], []
        for k in range(7):
            east.append(jnp.where(place >= 2**k, power, 0.0))
            west.append(jnp.where(place < LANES - 2**k, power, 0.0))
            power = power * power
        sums, ys, zs = [], [], []
        for c in range(chunks):
            v = mixed[:, c * LANES : (c + 1) * LANES]
            y = z = v
            for k in range(7):
                y = y + east[k] * pltpu.roll(y, 2**k, 1)
                z = z + west[k] * pltpu.roll(z, LANES - 2**k, 1)
            ys.append(column(y, LANES - 1))
            zs.append(column(z, 0))
            sums.append(y + z - v)
        carry = ys[0]
        for c in range(1, chunks):
            sums[c] = sums[c] + to_east * carry
            carry = ys[c] + stride * carry
        back = zs[chunks - 1]
        for c in range(chunks - 2, -1, -1):
            sums[c] = sums[c] + to_west * back
            back = zs[c] + stride * back
        for c in range(chunks):
            rows[q, :, here, c * LANES : (c + 1) * LANES] = sums[c].reshape(levels, SUB, LANES)
        edge = jnp.zeros((SUB, LANES), jnp.float32)
        lane = lane_of(edge)
        for t in range(levels):
            own = slice(t * SUB, (t + 1) * SUB)
            edge = jnp.where(lane == 2 * t, carry[own], jnp.where(lane == 2 * t + 1, back[own], edge))
        edges[q, here, :] = edge

    def find_state(q, h):
        here = part_rows(h)
        log = packed[0, q, here, :] * float(width)
        eastward = lax.rem(lane_of(log), 2) == 0
        total = edges[q, here, :] * jnp.exp(log * float(n_lon - 1))
        for step in range(1, n_lon):
            hops = jnp.where(eastward, float(step - 1), float(n_lon - step - 1))
            total = total + edges_in[q, step - 1, here, :] * jnp.exp(log * hops)
        state[...] = total / (1.0 - jnp.exp(log * float(n_lon)))

    def set_row(q, h, t, at, value):
        rows[q, t, part_rows(h), at] = value

    def set_own(q, h, at, value):
        gathered[q, part_gathered(h), at] = value

    def correct(q, h, t, store):
        here = part_rows(h)
        incoming = state[...]
        scale = spread_lane(packed[1, q, here, :], 2 * t)
        stride, to_east, to_west = powers(spread_lane(packed[0, q, here, :], 2 * t))
        carry = spread_lane(incoming, 2 * t) * scale
        back = spread_lane(incoming, 2 * t + 1) * scale
        pieces = []
        for c in range(chunks):
            pieces.append(scale * rows[q, t, here, c * LANES : (c + 1) * LANES] + to_east * carry)
            carry = carry * stride
        for c in range(chunks - 1, -1, -1):
            pieces[c] = pieces[c] + to_west * back
            back = back * stride
        for c in range(chunks):
            store(slice(c * LANES, (c + 1) * LANES), pieces[c])

    def first(unit, _):
        q, h = unit // parts, lax.rem(unit, parts)

        def scan(place, _):
            g = h * (groups // parts) + place

            @pl.when(q == 0)
            def _():
                field_copy(g).wait()

            scan_group(q, g)
            return 0

        lax.fori_loop(0, groups // parts, scan, 0)

        @pl.when(unit == 0)
        def _():
            pl.semaphore_wait(barrier, n_lon - 1 + n_lat - 1)

        for step in range(1, n_lon):
            edge_copy(q, h, step).start()
        for step in range(1, n_lon):
            edge_copy(q, h, step).wait()
        find_state(q, h)

        def ship(place, _):
            step = step_at(lat, place, n_lat)
            t = partner(lat, step, n_lat)
            correct(q, h, t, functools.partial(set_row, q, h, t))
            x_copy(q, h, step).start()
            return 0

        lax.fori_loop(0, n_lat - 1, ship, 0)
        correct(q, h, lat, functools.partial(set_own, q, h))
        return 0

    lax.fori_loop(0, rounds * parts, first, 0)
    weights_copy.wait()
    w_high[...], w_low[...] = split(weights[...])

    def second(q, _):
        for step in order:
            for h in range(parts):
                x_copy(q, h, step).wait_recv()
        tile = 256 if width % 256 == 0 else LANES

        def columns(n, _):
            at = pl.ds(pl.multiple_of(n * tile, tile), tile)
            smooth[q, :, at] = dot3(w_high[...], w_low[...], gathered[q, :, at])
            return 0

        lax.fori_loop(0, width // tile, columns, 0)

        def ship(place, _):
            y_copy(q, step_at(lat, place, n_lat)).start()
            return 0

        lax.fori_loop(0, n_lat - 1, ship, 0)
        own_copy(q).start()
        return 0

    lax.fori_loop(0, rounds, second, 0)

    def finish(q, _):
        own_copy(q).wait()
        for step in order:
            for h in range(parts):
                x_copy(q, h, step).wait_send()
            y_copy(q, step).wait()
        return 0

    lax.fori_loop(0, rounds, finish, 0)


def on_device(n_lon, n_lat, field, vertical, rate, lat_kernel):
    lev, depth, width = field.shape
    total = depth * n_lat
    rounds = lev // n_lat
    parts = 3 if depth % (3 * SUB) == 0 else 1
    f32, bf16 = jnp.float32, jnp.bfloat16
    pair = jnp.stack([jnp.log1p(-rate), rate / (2.0 - rate)])
    pair = pair.reshape(2, n_lat, rounds, depth).transpose(0, 2, 3, 1)
    packed = jnp.pad(jnp.repeat(pair, 2, axis=3), ((0, 0), (0, 0), (0, 0), (0, LANES - 2 * n_lat)), constant_values=-1.0)
    vmem, dma = pltpu.VMEM, pltpu.SemaphoreType.DMA
    return pl.pallas_call(
        functools.partial(kernel, n_lon, n_lat),
        out_shape=jax.ShapeDtypeStruct(field.shape, f32),
        in_specs=[
            pl.BlockSpec(memory_space=pl.ANY),
            pl.BlockSpec(memory_space=pltpu.VMEM),
            pl.BlockSpec(memory_space=pltpu.VMEM),
            pl.BlockSpec(memory_space=pl.ANY),
        ],
        out_specs=pl.BlockSpec(memory_space=pl.ANY),
        scratch_shapes=[
            vmem(field.shape, f32),
            vmem((total, total), f32),
            vmem((rounds, n_lat * SUB, lev * SUB), bf16),
            vmem((rounds, n_lat * SUB, lev * SUB), bf16),
            vmem((total, total), bf16),
            vmem((total, total), bf16),
            vmem((rounds, n_lat, depth, width), f32),
            vmem((rounds, depth, LANES), f32),
            vmem((rounds, n_lon - 1, depth, LANES), f32),
            vmem((depth // parts, LANES), f32),
            vmem((rounds, total, width), f32),
            vmem((rounds, total, width), f32),
            dma((rounds, parts, n_lon - 1)),
            dma((rounds, parts, n_lon - 1)),
            dma((rounds, parts, n_lat - 1)),
            dma((rounds, parts, n_lat - 1)),
            dma((rounds, n_lat - 1)),
            dma((rounds, n_lat - 1)),
            dma((rounds,)),
            dma((depth // SUB,)),
            dma(()),
        ],
        compiler_params=pltpu.CompilerParams(
            collective_id=0, has_side_effects=True, vmem_limit_bytes=60 * 1024 * 1024
        ),
        cost_estimate=pl.CostEstimate(
            flops=6 * lev * depth * width * (total + lev), bytes_accessed=8 * lev * depth * width, transcendentals=0
        ),
    )(field, vertical, packed, lat_kernel)


def solution(mesh):
    return jax.shard_map(
        functools.partial(on_device, mesh.shape["lon"], mesh.shape["lat"]),
        mesh=mesh,
        in_specs=(P(None, "lat", "lon"), P(), P(None, "lat"), P()),
        out_specs=P(None, "lat", "lon"),
        check_vma=False,
    )
```

```python
import functools

import jax
import jax.numpy as jnp
from jax import lax
from jax.experimental import pallas as pl
from jax.experimental.pallas import tpu as pltpu
from jax.sharding import PartitionSpec as P

MESH = pl.DeviceIdType.MESH
LANES = 128
SUB = 8


def partner(me, step, count):
    index, bit = 0, 1
    while bit < count:
        index = index + lax.rem(me // bit + step // bit, 2) * bit
        bit *= 2
    return index


def step_at(me, place, count):
    turn = lax.rem(me, count // 2)
    return lax.rem(place - turn + count - 1, count - 1) + 1


def split(value):
    high = value.astype(jnp.bfloat16)
    low = (value - high.astype(jnp.float32)).astype(jnp.bfloat16)
    return high, low


def dot3(a_high, a_low, b):
    high, low = split(b)
    dot = functools.partial(jnp.dot, preferred_element_type=jnp.float32)
    return dot(a_high, high) + (dot(a_high, low) + dot(a_low, high))


def kernel(
    n_lon, n_lat,
    field_hbm, vertical, packed, weights_hbm, out,
    field, weights, mix_high, mix_low, w_high, w_low, rows, edges, edges_in, state, gathered, smooth,
    edge_send, edge_recv, x_send, x_recv, y_send, y_recv, own_sem, field_sem, weights_sem,
):
    lon, lat = lax.axis_index("lon"), lax.axis_index("lat")
    rounds, levels, depth, width = rows.shape
    groups, chunks = depth // SUB, width // LANES
    parts = x_send.shape[1]
    part = depth // parts
    order = range(1, n_lat)

    barrier = pltpu.get_barrier_semaphore()
    for step in range(1, n_lon):
        pl.semaphore_signal(barrier, inc=1, device_id={"lon": lax.rem(lon + step, n_lon)}, device_id_type=MESH)
    for step in order:
        pl.semaphore_signal(barrier, inc=1, device_id={"lat": partner(lat, step, n_lat)}, device_id_type=MESH)

    def group_rows(g):
        return pl.ds(pl.multiple_of(g * SUB, SUB), SUB)

    def part_rows(h):
        return pl.ds(pl.multiple_of(h * part, SUB), part)

    def part_gathered(h):
        return pl.ds(pl.multiple_of(lat * depth + h * part, SUB), part)

    def edge_copy(q, h, step):
        return pltpu.make_async_remote_copy(
            src_ref=edges.at[q, part_rows(h)], dst_ref=edges_in.at[q, step - 1, part_rows(h)],
            send_sem=edge_send.at[q, h, step - 1], recv_sem=edge_recv.at[q, h, step - 1],
            device_id={"lon": lax.rem(lon + step, n_lon)}, device_id_type=MESH,
        )

    def x_copy(q, h, step):
        target = partner(lat, step, n_lat)
        return pltpu.make_async_remote_copy(
            src_ref=rows.at[q, target, part_rows(h)], dst_ref=gathered.at[q, part_gathered(h)],
            send_sem=x_send.at[q, h, step - 1], recv_sem=x_recv.at[q, h, step - 1],
            device_id={"lat": target}, device_id_type=MESH,
        )

    def y_copy(q, step):
        target = partner(lat, step, n_lat)
        return pltpu.make_async_remote_copy(
            src_ref=smooth.at[q, pl.ds(pl.multiple_of(target * depth, SUB), depth)],
            dst_ref=out.at[lat * rounds + q],
            send_sem=y_send.at[q, step - 1], recv_sem=y_recv.at[q, step - 1],
            device_id={"lat": target}, device_id_type=MESH,
        )

    def own_copy(q):
        return pltpu.make_async_copy(
            smooth.at[q, pl.ds(pl.multiple_of(lat * depth, SUB), depth)],
            out.at[lat * rounds + q], own_sem.at[q],
        )

    def field_copy(g):
        return pltpu.make_async_copy(
            field_hbm.at[:, group_rows(g), :], field.at[:, group_rows(g), :], field_sem.at[g]
        )

    def load(g, _):
        field_copy(g).start()
        return 0

    weights_copy = pltpu.make_async_copy(weights_hbm, weights, weights_sem)
    lax.fori_loop(0, groups, load, 0)
    weights_copy.start()

    wide, lev = levels * SUB, vertical.shape[0]
    one_hot = lambda hit: jnp.where(hit, 1.0, 0.0).astype(jnp.bfloat16)
    dot = functools.partial(jnp.dot, preferred_element_type=jnp.float32)
    iota = lambda shape, axis: lax.broadcasted_iota(jnp.int32, shape, axis)
    spread = one_hot(iota((lev, lev * SUB), 0) == lax.shift_right_logical(iota((lev, lev * SUB), 1), 3))
    grid = (wide, lev * SUB)
    same = lax.bitwise_and(iota(grid, 0), SUB - 1) == lax.bitwise_and(iota(grid, 1), SUB - 1)
    for q in range(rounds):
        chosen = one_hot(lax.shift_right_logical(iota((wide, lev), 0), 3) * rounds + q == iota((wide, lev), 1))
        for half, target in zip(split(vertical[...]), (mix_high, mix_low)):
            picked = dot(chosen, half).astype(jnp.bfloat16)
            target[q] = jnp.where(same, dot(picked, spread), 0.0).astype(jnp.bfloat16)

    def spread_lane(values, index):
        one = jnp.sum(jnp.where(lane_of(values) == index, values, 0.0), axis=1, keepdims=True)
        return jnp.broadcast_to(one, values.shape)

    def lane_of(values):
        return lax.broadcasted_iota(jnp.int32, values.shape, 1)

    def column(values, index):
        return jnp.broadcast_to(values[:, index : index + 1], values.shape)

    def powers(log):
        place = lane_of(log)
        ahead = (place + 1).astype(jnp.float32)
        behind = (LANES - place).astype(jnp.float32)
        return jnp.exp(log * float(LANES)), jnp.exp(log * ahead), jnp.exp(log * behind)

    def scan_group(q, g):
        here = group_rows(g)
        x = field[:, here, :]
        x = x.reshape(x.shape[0] * SUB, width)
        mixed = dot3(mix_high[q], mix_low[q], x)
        logs = packed[0, q, here, :]
        log = jnp.concatenate([spread_lane(logs, 2 * t) for t in range(levels)], axis=0)
        stride, to_east, to_west = powers(log)
        place = lane_of(log)
        power = jnp.exp(log)
        east, west = [], []
        for k in range(7):
            east.append(jnp.where(place >= 2**k, power, 0.0))
            west.append(jnp.where(place < LANES - 2**k, power, 0.0))
            power = power * power
        sums, ys, zs = [], [], []
        for c in range(chunks):
            v = mixed[:, c * LANES : (c + 1) * LANES]
            y = z = v
            for k in range(7):
                y = y + east[k] * pltpu.roll(y, 2**k, 1)
                z = z + west[k] * pltpu.roll(z, LANES - 2**k, 1)
            ys.append(column(y, LANES - 1))
            zs.append(column(z, 0))
            sums.append(y + z - v)
        carry = ys[0]
        for c in range(1, chunks):
            sums[c] = sums[c] + to_east * carry
            carry = ys[c] + stride * carry
        back = zs[chunks - 1]
        for c in range(chunks - 2, -1, -1):
            sums[c] = sums[c] + to_west * back
            back = zs[c] + stride * back
        for c in range(chunks):
            rows[q, :, here, c * LANES : (c + 1) * LANES] = sums[c].reshape(levels, SUB, LANES)
        edge = jnp.zeros((SUB, LANES), jnp.float32)
        lane = lane_of(edge)
        for t in range(levels):
            own = slice(t * SUB, (t + 1) * SUB)
            edge = jnp.where(lane == 2 * t, carry[own], jnp.where(lane == 2 * t + 1, back[own], edge))
        edges[q, here, :] = edge

    def find_state(q, h):
        here = part_rows(h)
        log = packed[0, q, here, :] * float(width)
        eastward = lax.rem(lane_of(log), 2) == 0
        total = edges[q, here, :] * jnp.exp(log * float(n_lon - 1))
        for step in range(1, n_lon):
            hops = jnp.where(eastward, float(step - 1), float(n_lon - step - 1))
            total = total + edges_in[q, step - 1, here, :] * jnp.exp(log * hops)
        state[...] = total / (1.0 - jnp.exp(log * float(n_lon)))

    def set_row(q, h, t, at, value):
        rows[q, t, part_rows(h), at] = value

    def set_own(q, h, at, value):
        gathered[q, part_gathered(h), at] = value

    def correct(q, h, t, store):
        here = part_rows(h)
        incoming = state[...]
        scale = spread_lane(packed[1, q, here, :], 2 * t)
        stride, to_east, to_west = powers(spread_lane(packed[0, q, here, :], 2 * t))
        carry = spread_lane(incoming, 2 * t) * scale
        back = spread_lane(incoming, 2 * t + 1) * scale
        pieces = []
        for c in range(chunks):
            pieces.append(scale * rows[q, t, here, c * LANES : (c + 1) * LANES] + to_east * carry)
            carry = carry * stride
        for c in range(chunks - 1, -1, -1):
            pieces[c] = pieces[c] + to_west * back
            back = back * stride
        for c in range(chunks):
            store(slice(c * LANES, (c + 1) * LANES), pieces[c])

    def first(unit, _):
        q, h = unit // parts, lax.rem(unit, parts)

        def scan(place, _):
            g = h * (groups // parts) + place

            @pl.when(q == 0)
            def _():
                field_copy(g).wait()

            scan_group(q, g)
            return 0

        lax.fori_loop(0, groups // parts, scan, 0)

        @pl.when(unit == 0)
        def _():
            pl.semaphore_wait(barrier, n_lon - 1 + n_lat - 1)

        for step in range(1, n_lon):
            edge_copy(q, h, step).start()
        for step in range(1, n_lon):
            edge_copy(q, h, step).wait()
        find_state(q, h)

        def ship(place, _):
            step = step_at(lat, place, n_lat)
            t = partner(lat, step, n_lat)
            correct(q, h, t, functools.partial(set_row, q, h, t))
            x_copy(q, h, step).start()
            return 0

        lax.fori_loop(0, n_lat - 1, ship, 0)
        correct(q, h, lat, functools.partial(set_own, q, h))
        return 0

    lax.fori_loop(0, rounds * parts, first, 0)
    weights_copy.wait()
    w_high[...], w_low[...] = split(weights[...])

    def second(q, _):
        for step in order:
            for h in range(parts):
                x_copy(q, h, step).wait_recv()
        tile = 256 if width % 256 == 0 else LANES

        def columns(n, _):
            at = pl.ds(pl.multiple_of(n * tile, tile), tile)
            smooth[q, :, at] = dot3(w_high[...], w_low[...], gathered[q, :, at])
            return 0

        lax.fori_loop(0, width // tile, columns, 0)

        def ship(place, _):
            y_copy(q, step_at(lat, place, n_lat)).start()
            return 0

        lax.fori_loop(0, n_lat - 1, ship, 0)
        own_copy(q).start()
        return 0

    lax.fori_loop(0, rounds, second, 0)

    def finish(q, _):
        own_copy(q).wait()
        for step in order:
            for h in range(parts):
                x_copy(q, h, step).wait_send()
            y_copy(q, step).wait()
        return 0

    lax.fori_loop(0, rounds, finish, 0)


def write_out(landed, out, sems):
    count = sems.shape[0]
    size = out.shape[0] // count
    copies = [
        pltpu.make_async_copy(landed.at[pl.ds(i * size, size)], out.at[pl.ds(i * size, size)], sems.at[i])
        for i in range(count)
    ]
    for copy in copies:
        copy.start()
    for copy in copies:
        copy.wait()


def on_device(n_lon, n_lat, field, vertical, rate, lat_kernel):
    lev, depth, width = field.shape
    total = depth * n_lat
    rounds = lev // n_lat
    parts = 3 if depth % (3 * SUB) == 0 else 1
    f32, bf16 = jnp.float32, jnp.bfloat16
    pair = jnp.stack([jnp.log1p(-rate), rate / (2.0 - rate)])
    pair = pair.reshape(2, n_lat, rounds, depth).transpose(0, 2, 3, 1)
    packed = jnp.pad(jnp.repeat(pair, 2, axis=3), ((0, 0), (0, 0), (0, 0), (0, LANES - 2 * n_lat)), constant_values=-1.0)
    vmem, dma = pltpu.VMEM, pltpu.SemaphoreType.DMA
    landed = pl.pallas_call(
        functools.partial(kernel, n_lon, n_lat),
        out_shape=pltpu.VMEM(field.shape, f32),
        in_specs=[
            pl.BlockSpec(memory_space=pl.ANY),
            pl.BlockSpec(memory_space=pltpu.VMEM),
            pl.BlockSpec(memory_space=pltpu.VMEM),
            pl.BlockSpec(memory_space=pl.ANY),
        ],
        out_specs=pl.BlockSpec(memory_space=pltpu.VMEM),
        scratch_shapes=[
            vmem(field.shape, f32),
            vmem((total, total), f32),
            vmem((rounds, n_lat * SUB, lev * SUB), bf16),
            vmem((rounds, n_lat * SUB, lev * SUB), bf16),
            vmem((total, total), bf16),
            vmem((total, total), bf16),
            vmem((rounds, n_lat, depth, width), f32),
            vmem((rounds, depth, LANES), f32),
            vmem((rounds, n_lon - 1, depth, LANES), f32),
            vmem((depth // parts, LANES), f32),
            vmem((rounds, total, width), f32),
            vmem((rounds, total, width), f32),
            dma((rounds, parts, n_lon - 1)),
            dma((rounds, parts, n_lon - 1)),
            dma((rounds, parts, n_lat - 1)),
            dma((rounds, parts, n_lat - 1)),
            dma((rounds, n_lat - 1)),
            dma((rounds, n_lat - 1)),
            dma((rounds,)),
            dma((depth // SUB,)),
            dma(()),
        ],
        compiler_params=pltpu.CompilerParams(
            collective_id=0, has_side_effects=True, vmem_limit_bytes=50 * 1024 * 1024
        ),
        cost_estimate=pl.CostEstimate(
            flops=6 * lev * depth * width * (total + lev), bytes_accessed=8 * lev * depth * width, transcendentals=0
        ),
    )(field, vertical, packed, lat_kernel)
    return pl.pallas_call(
        write_out,
        out_shape=jax.ShapeDtypeStruct(field.shape, f32),
        in_specs=[pl.BlockSpec(memory_space=pltpu.VMEM)],
        out_specs=pl.BlockSpec(memory_space=pl.ANY),
        scratch_shapes=[dma((rounds,))],
        compiler_params=pltpu.CompilerParams(vmem_limit_bytes=12 * 1024 * 1024),
        cost_estimate=pl.CostEstimate(flops=0, bytes_accessed=8 * lev * depth * width, transcendentals=0),
    )(landed)


def solution(mesh):
    return jax.shard_map(
        functools.partial(on_device, mesh.shape["lon"], mesh.shape["lat"]),
        mesh=mesh,
        in_specs=(P(None, "lat", "lon"), P(), P(None, "lat"), P()),
        out_specs=P(None, "lat", "lon"),
        check_vma=False,
    )
```
